32 devices in a mesh: groups: 2 (over x), owner: 16 (over z, y, core).
Axes of the slice: x: 2, y: 2, z: 4, core: 2. Of those that a mesh axis runs over, the one named last changes fastest.
Arguments:
- queries: bfloat16 [512, 8192], P(('groups', 'owner')), parts along dimension 0, may hold values from -12 to 12
- request_prefix: int32 [512, 1], P(('groups', 'owner')), parts along dimension 0, may hold values from 0 to 15; in each aligned block of 16 rows (0 to 15, 16 to 31, ...) at most 2 rows name the same one
- suffix_len: int32 [512], P(('groups', 'owner')), parts along dimension 0, may hold values from 1 to 32, 4096 in all
- block_map: int32 [64], P('groups'), parts along dimension 0, may hold values from 0 to 31, each once
- prefix_keys: bfloat16 [64, 1024, 1024], P(('groups', 'owner')), parts along dimension 0, may hold values from -12 to 12
- prefix_values: bfloat16 [64, 1024, 1024], P(('groups', 'owner')), parts along dimension 0, may hold values from -10 to 10
- suffix_keys: bfloat16 [512, 32, 1024], P(('groups', 'owner')), parts along dimension 0, may hold values from -12 to 12
- suffix_values: bfloat16 [512, 32, 1024], P(('groups', 'owner')), parts along dimension 0, may hold values from -10 to 10
Outputs:
- attended: bfloat16 [512, 8192], P(('groups', 'owner')), parts along dimension 0
The draws below stay inside these ranges and needn't reach their ends.
There are 2 independent parts, one for each index of `groups`. The reference program is written for one: setup_inputs(seed, part) draws one part's arguments, and reference() takes and returns one part's arrays. A program takes and returns all parts, laid end to end along the dimension named above; each array names one. Nothing has to cross between parts.
Inputs may be any that keep to these rules, and one draw needn't show every extreme that they name: `request_prefix`: at most 2 requests of one device continue the same prefix. `block_map`: each slot appears once; slot s lies on owner s // 2.
All inputs are finite; a program needn't handle non-finite values. No bound on the sum of `suffix_len` on one device may be relied on, other than what follows from the above.
Results may differ from the reference program's by a relative error of at most 0.0043.
Values may be sent and summed in bfloat16 or wider, within the bound.
A program may use at most 128 MiB of HBM per device.

```python
import math
import jax
import jax.numpy as jnp
import numpy as np
from jax import lax

HEADS = 64
KV_HEADS = 8
HEAD_DIM = 128
REQ_DEV = 16
SPAN = 1024
PREFIXES = 16
CAP = 2
SUF = 32
REQUESTS = 256
SLOTS = 32
CPP = 2


def draw_queries(key, part):
    shape = (REQUESTS, HEADS * HEAD_DIM)
    noise = 1.5 * jax.random.normal(jax.random.fold_in(key, 103), shape, jnp.float32)
    return jnp.clip(noise, -12.0, 12.0).astype(jnp.bfloat16)


def draw_prefix_keys(key, part):
    shape = (SLOTS, SPAN, KV_HEADS * HEAD_DIM)
    noise = 1.5 * jax.random.normal(jax.random.fold_in(key, 203), shape, jnp.float32)
    return jnp.clip(noise, -12.0, 12.0).astype(jnp.bfloat16)


def steps_of(own_key, shape, cuts, low, largest):
    loudness, own = 1.0, jax.random.fold_in(own_key, 6)
    for axis_at, shards_of in cuts:
        steps = jnp.exp(jax.random.uniform(jax.random.fold_in(own, axis_at), (shards_of,), jnp.float32, low / len(cuts), largest / len(cuts)))
        loudness = loudness * jnp.repeat(steps, shape[axis_at] // shards_of).reshape([-1 if axis == axis_at else 1 for axis in range(len(shape))])
    return loudness


def length_profile(number_of, total, reach, slope):
    loads = [(1 << 20) // math.isqrt(standing ** slope) + 1 for standing in range(2, number_of + 1)]
    surplus, given = total - reach - (number_of - 1), [1] * (number_of - 1)
    while surplus > 0:
        candidates = [i for i in range(number_of - 1) if given[i] < reach]
        whole, remaining = sum([loads[i] for i in candidates]), surplus
        for i in candidates:
            addition = min(reach - given[i], max(1, remaining * loads[i] // whole), surplus)
            given[i] = given[i] + addition
            surplus = surplus - addition
    return np.array([reach] + given)


def ragged(own_key, amount, total, most, lean):
    if amount == 2:
        one = jax.random.randint(own_key, (), max(1, total - most), min(most, total - 1) + 1)
        return jnp.stack([one, total - one])
    tallies = jnp.asarray(length_profile(amount, total, most, lean), jnp.int32)
    twos = (amount - 1) // 2
    giver, taker = tallies[1:1 + 2 * twos:2], tallies[2:2 + 2 * twos:2]
    room = jnp.minimum(giver - 1, most - taker)
    moved = jax.random.randint(jax.random.fold_in(own_key, 1), (twos,), 0, 1 << 20) % (room + 1)
    tallies = tallies.at[1:1 + 2 * twos:2].set(giver - moved).at[2:2 + 2 * twos:2].set(taker + moved)
    return tallies[jax.random.permutation(jax.random.fold_in(own_key, 2), amount)]


def deal_out(key, own, number, rows, count, top, most, lean):
    ranking = jax.random.permutation(key, count)
    packed, common = portions_of(count, rows * top, most, lean, True), portions_of(count, rows * top, most, lean, False)
    places = jnp.arange(count)

    def named(sizes, rotation):
        used = int((sizes > 0).sum())
        fixed = max(1, used // 4)
        shifted = fixed + (places - fixed + rotation * (used - fixed)) % max(1, count - fixed)
        return jnp.zeros((count,), jnp.int32).at[ranking[jnp.where(places < fixed, places, shifted)]].set(jnp.asarray(sizes, jnp.int32))

    sizes = jnp.where(number % 4 == 0, named(packed, number // 4), named(common, number - number // 4 - 1))
    mixed = jax.random.permutation(jax.random.fold_in(own, 3), count)
    donor, receiver = mixed[0:count // 2 * 2:2], mixed[1:count // 2 * 2:2]
    room = jnp.minimum(sizes[donor] - 1, most - sizes[receiver]) // 2
    room = jnp.where((donor == ranking[0]) | (receiver == ranking[0]) | (sizes[receiver] == 0), 0, jnp.maximum(room, 0))
    shifted = jax.random.randint(jax.random.fold_in(own, 4), (count // 2,), 0, 1 << 20) % (room + 1)
    sizes = sizes.at[donor].add(-shifted).at[receiver].add(shifted)
    labels = jnp.searchsorted(jnp.cumsum(sizes), jnp.arange(rows * top), side="right").astype(jnp.int32)
    grid = labels.reshape(top, rows).T
    grid = grid[jax.random.permutation(jax.random.fold_in(own, 1), rows)]
    rotation = jax.random.randint(jax.random.fold_in(own, 2), (rows, 1), 0, top)
    return jnp.take_along_axis(grid, (jnp.arange(top)[None, :] + rotation) % top, axis=1)


def portions_of(number_of, total, reach, slope, full):
    portions = [(1 << 20) // math.isqrt(grade ** slope) + 1 for grade in range(1, number_of + 1)]
    largest = reach if full else min(reach, max(-(-total // number_of), total * portions[0] // sum(portions)))
    least = 1 if total - largest >= number_of - 1 else 0
    counts, spare = [largest] + [least] * (number_of - 1), total - largest - least * (number_of - 1)
    while spare > 0:
        candidates = [i for i in range(1, number_of) if counts[i] < largest] or [i for i in range(1, number_of) if counts[i] < reach]
        pool, remaining = sum([portions[i] for i in candidates]), spare
        for i in candidates:
            more = min(reach - counts[i], max(1, remaining * portions[i] // pool), spare)
            counts[i] = counts[i] + more
            spare = spare - more
    return np.array(counts)


def normal_values(key, shape, spread, most, pieces=(), held_as=jnp.bfloat16):
    loudness = steps_of(key, shape, pieces, -0.22, 0.18) if pieces else 1.0
    entries = jax.random.normal(key, shape, jnp.float32) * spread * loudness
    return jnp.minimum(jnp.maximum(entries, -most), most).astype(held_as)


def setup_inputs(seed: int = 0, part: int = 0) -> dict:
    arg_keys = jax.random.split(jax.random.key(seed), 9)
    part_keys = jax.random.split(jax.random.fold_in(arg_keys[8], part), 9)
    queries = draw_queries(jax.random.fold_in(jax.random.fold_in(arg_keys[8], part), 71), part)
    request_prefix_keys = jax.random.split(jax.random.fold_in(part_keys[1], 1), REQUESTS // REQ_DEV)
    request_prefix_turns = jax.random.permutation(jax.random.fold_in(part_keys[1], 3), REQUESTS // REQ_DEV)
    request_prefix = jax.vmap(lambda own, number: deal_out(jax.random.fold_in(part_keys[1], 2), own, number, REQ_DEV, PREFIXES, 1, CAP, 2))(request_prefix_keys, request_prefix_turns).reshape((REQUESTS, 1))
    suffix_len = ragged(part_keys[2], REQUESTS, REQUESTS * SUF // 2, SUF, 1).astype(jnp.int32)
    block_map = jax.random.permutation(part_keys[3], SLOTS).astype(jnp.int32)
    prefix_keys = draw_prefix_keys(jax.random.fold_in(jax.random.fold_in(arg_keys[8], part), 71), part)
    prefix_values = normal_values(part_keys[5], (SLOTS, SPAN, KV_HEADS * HEAD_DIM), 2.0, 10.0, ((0, 16),))
    suffix_keys = normal_values(part_keys[6], (REQUESTS, SUF, KV_HEADS * HEAD_DIM), 3.0, 12.0, ((0, 16),))
    suffix_values = normal_values(part_keys[7], (REQUESTS, SUF, KV_HEADS * HEAD_DIM), 2.0, 10.0, ((0, 16),))
    return dict(queries=queries, request_prefix=request_prefix, suffix_len=suffix_len, block_map=block_map, prefix_keys=prefix_keys, prefix_values=prefix_values, suffix_keys=suffix_keys, suffix_values=suffix_values)


NEG_FILL = -1e+30

def prefix_terms(query_row, prefix_id, block_map, prefix_keys, prefix_values):
    per_group = HEADS // KV_HEADS
    span_ids = (prefix_id * CPP + jnp.arange(CPP, dtype=jnp.int32)).astype(jnp.int32)
    slot_ids = jnp.take(block_map, span_ids).astype(jnp.int32)
    key_block = jnp.take(prefix_keys, slot_ids, axis=0).astype(jnp.float32).reshape(CPP, SPAN, KV_HEADS, HEAD_DIM)
    value_block = jnp.take(prefix_values, slot_ids, axis=0).astype(jnp.float32).reshape(CPP, SPAN, KV_HEADS, HEAD_DIM)
    query_heads = query_row.astype(jnp.float32).reshape(KV_HEADS, per_group, HEAD_DIM)
    scores = jnp.einsum('hgd,cthd->chgt', query_heads, key_block) * (1.0 / math.sqrt(HEAD_DIM))
    highest = lax.optimization_barrier(jnp.max(scores, axis=-1, keepdims=True))
    expon = jnp.exp(scores - highest)
    summed = lax.optimization_barrier(jnp.sum(expon, axis=-1))
    weights = lax.optimization_barrier(expon.astype(jnp.bfloat16)).astype(jnp.float32)
    mixed = jnp.einsum('chgt,cthd->chgd', weights, value_block) / summed[..., None]
    span_out = mixed.astype(jnp.bfloat16).reshape(CPP, HEADS, HEAD_DIM)
    span_lse = (highest[..., 0] + jnp.log(summed)).reshape(CPP, HEADS)
    return (span_out, span_lse)

def suffix_terms(queries, suffix_keys, suffix_values, suffix_len):
    row_count = queries.shape[0]
    per_group = HEADS // KV_HEADS
    query_heads = queries.astype(jnp.float32).reshape(row_count, KV_HEADS, per_group, HEAD_DIM)
    key_heads = suffix_keys.astype(jnp.float32).reshape(row_count, SUF, KV_HEADS, HEAD_DIM)
    value_heads = suffix_values.astype(jnp.float32).reshape(row_count, SUF, KV_HEADS, HEAD_DIM)
    scores = jnp.einsum('rhgd,rthd->rhgt', query_heads, key_heads) * (1.0 / math.sqrt(HEAD_DIM))
    visible = (jnp.arange(SUF, dtype=jnp.int32)[None, :] < suffix_len[:, None])[:, None, None, :]
    highest = lax.optimization_barrier(jnp.max(jnp.where(visible, scores, NEG_FILL), axis=-1, keepdims=True))
    expon = jnp.where(visible, jnp.exp(scores - highest), 0.0)
    summed = lax.optimization_barrier(jnp.sum(expon, axis=-1))
    weights = lax.optimization_barrier(expon.astype(jnp.bfloat16)).astype(jnp.float32)
    mixed = jnp.einsum('rhgt,rthd->rhgd', weights, value_heads) / summed[..., None]
    suffix_out = mixed.reshape(row_count, HEADS, HEAD_DIM)
    suffix_lse = (highest[..., 0] + jnp.log(summed)).reshape(row_count, HEADS)
    return (suffix_out, suffix_lse)

def combine_terms(span_out, span_lse, suffix_out, suffix_lse):
    row_count = span_out.shape[0]
    highest = jnp.maximum(lax.optimization_barrier(jnp.max(span_lse, axis=1)), suffix_lse)
    span_scale = jnp.exp(span_lse - highest[:, None, :])
    suffix_scale = jnp.exp(suffix_lse - highest)
    numerator = lax.optimization_barrier(jnp.sum(span_scale[..., None] * span_out.astype(jnp.float32), axis=1)) + suffix_scale[..., None] * suffix_out
    denominator = lax.optimization_barrier(jnp.sum(span_scale, axis=1)) + suffix_scale
    return (numerator / denominator[..., None]).astype(jnp.bfloat16).reshape(row_count, HEADS * HEAD_DIM)

def reference(queries, request_prefix, suffix_len, block_map, prefix_keys, prefix_values, suffix_keys, suffix_values):
    prefix_ids = request_prefix[:, 0].astype(jnp.int32)

    def per_request(pair):
        query_row, prefix_id = pair
        return prefix_terms(query_row, prefix_id, block_map, prefix_keys, prefix_values)
    span_out, span_lse = lax.map(per_request, (queries, prefix_ids))
    suffix_out, suffix_lse = suffix_terms(queries, suffix_keys, suffix_values, suffix_len)
    return combine_terms(span_out, span_lse, suffix_out, suffix_lse)
```

```python
import functools
import math

import jax
import jax.numpy as jnp
from jax import lax
from jax.experimental import pallas as pl
from jax.experimental.pallas import tpu as pltpu
from jax.sharding import PartitionSpec as P

HEADS = 64
KV_HEADS = 8
HEAD_DIM = 128
PREFIXES = 16
CAP = 2
GROUP = HEADS // KV_HEADS
PAIR = 2
FACTOR = 1.0 / math.sqrt(HEAD_DIM)
LOG2E = math.log2(math.e)
NEG_FILL = -1e30
VMEM_LIMIT = 48 * 1024 * 1024


def row_positions(prefix_ref, map_ref, count_ref, rows, per_prefix, visit):
    for p in range(PREFIXES):
        count_ref[p] = 0
    for r in range(rows):
        p = prefix_ref[r]
        rank = count_ref[p]
        count_ref[p] = rank + 1
        for c in range(per_prefix):
            visit(r, c, map_ref[p * per_prefix + c] * CAP + rank)


def dispatch_kernel(prefix_ref, map_ref, q_ref, out_ref, count_ref):
    out_ref[...] = jnp.zeros_like(out_ref)

    def visit(r, c, pos):
        out_ref[pos] = q_ref[r]

    row_positions(
        prefix_ref, map_ref, count_ref, q_ref.shape[0], map_ref.shape[0] // PREFIXES, visit
    )


def span_kernel(q_ref, k_ref, v_ref, out_ref, lse_ref, *, sources, slots, chunk):
    step = pl.program_id(0)

    @pl.when(step == 0)
    def _():
        lse_ref[...] = jnp.zeros_like(lse_ref)

    heads = PAIR * GROUP
    per = chunk * CAP
    for first in range(0, sources, chunk):
        for slot in range(slots):
            q = q_ref[pl.ds(first, chunk), slot].astype(jnp.float32).reshape(per, heads, HEAD_DIM)
            outs = []
            lses = []
            for j in range(PAIR):
                cols = slice(j * HEAD_DIM, (j + 1) * HEAD_DIM)
                qj = q[:, j * GROUP : (j + 1) * GROUP].reshape(per * GROUP, HEAD_DIM)
                raw = lax.dot_general(
                    qj.astype(jnp.bfloat16),
                    k_ref[slot, :, cols],
                    (((1,), (1,)), ((), ())),
                    preferred_element_type=jnp.float32,
                )
                highest = jnp.max(raw, axis=-1, keepdims=True)
                expon = jnp.exp2((raw - highest) * (FACTOR * LOG2E))
                total = jnp.sum(expon, axis=-1, keepdims=True)
                mixed = jnp.dot(
                    expon.astype(jnp.bfloat16),
                    v_ref[slot, :, cols],
                    preferred_element_type=jnp.float32,
                )
                outs.append((mixed / total).reshape(per, GROUP, HEAD_DIM))
                lse = highest * FACTOR + jnp.log(total)
                lses.append(
                    jnp.broadcast_to(lse, (per * GROUP, HEAD_DIM)).reshape(per, GROUP, HEAD_DIM)
                )
            shape = (per, heads, HEAD_DIM)
            out_ref[pl.ds(first, chunk), slot] = (
                jnp.concatenate(outs, axis=1)
                .astype(jnp.bfloat16)
                .reshape(chunk, CAP, heads, HEAD_DIM)
            )
            own = lax.broadcasted_iota(jnp.int32, shape, 2) == (
                lax.broadcasted_iota(jnp.int32, shape, 1) + step * heads
            )
            placed = jnp.sum(jnp.where(own, jnp.concatenate(lses, axis=1), 0.0), axis=1)
            lse_ref[slot, pl.ds(first * CAP, per)] += placed


def finish_kernel(
    prefix_ref,
    map_ref,
    len_ref,
    q_ref,
    sk_ref,
    sv_ref,
    back_ref,
    lse_ref,
    out_ref,
    count_ref,
    sel_ref,
    sel_lse_ref,
):
    step = pl.program_id(0)
    rows = q_ref.shape[0]
    per_prefix = map_ref.shape[0] // PREFIXES
    heads = PAIR * GROUP
    tokens = sk_ref.shape[0]
    room = tokens // rows

    def visit(r, c, pos):
        sel_ref[c, r] = back_ref[pos]
        sel_lse_ref[c, pl.ds(r, 1)] = lse_ref[pl.ds(pos, 1)]

    row_positions(prefix_ref, map_ref, count_ref, rows, per_prefix, visit)

    col = lax.broadcasted_iota(jnp.int32, (1, tokens), 1)
    limit = jnp.zeros((1, tokens), jnp.int32)
    for r in range(rows):
        limit = jnp.where(col // room == r, r * room + len_ref[r], limit)
    owner_row = lax.broadcasted_iota(jnp.int32, (rows * GROUP, tokens), 0) // GROUP
    visible = (owner_row == col // room) & (col < limit)
    q = q_ref[...].astype(jnp.float32)
    results = []
    lane = lax.broadcasted_iota(jnp.int32, (rows, GROUP, HEAD_DIM), 2)
    within = lax.broadcasted_iota(jnp.int32, (rows, GROUP, HEAD_DIM), 1)
    for j in range(PAIR):
        cols = slice(j * HEAD_DIM, (j + 1) * HEAD_DIM)
        part = slice(j * GROUP, (j + 1) * GROUP)
        qj = q[:, part].reshape(rows * GROUP, HEAD_DIM).astype(jnp.bfloat16)
        raw = lax.dot_general(
            qj, sk_ref[:, cols], (((1,), (1,)), ((), ())), preferred_element_type=jnp.float32
        )
        raw = jnp.where(visible, raw, NEG_FILL)
        highest = jnp.max(raw, axis=-1, keepdims=True)
        expon = jnp.where(visible, jnp.exp2((raw - highest) * (FACTOR * LOG2E)), 0.0)
        total = jnp.sum(expon, axis=-1, keepdims=True)
        mixed = jnp.dot(
            expon.astype(jnp.bfloat16), sv_ref[:, cols], preferred_element_type=jnp.float32
        )
        suffix_out = (mixed / total).reshape(rows, GROUP, HEAD_DIM)
        suffix_lse = (highest * FACTOR + jnp.log(total)).reshape(rows, GROUP, 1)
        mine = lane == within + (step * heads + j * GROUP)
        span_lse = []
        top = suffix_lse
        for c in range(per_prefix):
            wide = jnp.broadcast_to(sel_lse_ref[c][:, None, :], (rows, GROUP, HEAD_DIM))
            one = jnp.sum(jnp.where(mine, wide, 0.0), axis=-1, keepdims=True)
            span_lse.append(one)
            top = jnp.maximum(top, one)
        scale = jnp.exp(suffix_lse - top)
        numerator = scale * suffix_out
        denominator = scale
        for c in range(per_prefix):
            scale = jnp.exp(span_lse[c] - top)
            numerator += scale * sel_ref[c].astype(jnp.float32)[:, part]
            denominator += scale
        results.append(numerator / denominator)
    out_ref[...] = jnp.concatenate(results, axis=1).astype(jnp.bfloat16)


def body(
    queries,
    request_prefix,
    suffix_len,
    block_map,
    prefix_keys,
    prefix_values,
    suffix_keys,
    suffix_values,
):
    owners = lax.axis_size("owner")
    rows = queries.shape[0]
    slot_count = block_map.shape[0]
    slots, span, width = prefix_keys.shape
    per_prefix = slot_count // PREFIXES
    buffer = slot_count * CAP
    heads = PAIR * GROUP
    steps = HEADS // heads
    cols = PAIR * HEAD_DIM
    params = pltpu.CompilerParams(vmem_limit_bytes=VMEM_LIMIT)
    smem = pl.BlockSpec(memory_space=pltpu.SMEM)
    vmem = pl.BlockSpec(memory_space=pltpu.VMEM)
    prefix_ids = request_prefix.reshape(rows)
    q3 = queries.reshape(rows, HEADS, HEAD_DIM)

    outgoing = pl.pallas_call(
        dispatch_kernel,
        out_shape=jax.ShapeDtypeStruct((buffer, HEADS, HEAD_DIM), jnp.bfloat16),
        in_specs=[smem, smem, vmem],
        out_specs=vmem,
        scratch_shapes=[pltpu.SMEM((PREFIXES,), jnp.int32)],
        compiler_params=params,
        name="dispatch",
    )(prefix_ids, block_map, q3)
    received = lax.all_to_all(outgoing, "owner", split_axis=0, concat_axis=0, tiled=True)

    chunk = math.gcd(owners, 16)
    block = (owners, slots, CAP, heads, HEAD_DIM)
    row_spec = pl.BlockSpec(block, lambda i: (0, 0, 0, i, 0))
    kv_spec = pl.BlockSpec((slots, span, cols), lambda i: (0, 0, i))
    part_out, part_lse = pl.pallas_call(
        functools.partial(span_kernel, sources=owners, slots=slots, chunk=chunk),
        grid=(steps,),
        out_shape=(
            jax.ShapeDtypeStruct((owners, slots, CAP, HEADS, HEAD_DIM), jnp.bfloat16),
            jax.ShapeDtypeStruct((slots, owners * CAP, HEAD_DIM), jnp.float32),
        ),
        in_specs=[row_spec, kv_spec, kv_spec],
        out_specs=(
            row_spec,
            pl.BlockSpec((slots, owners * CAP, HEAD_DIM), lambda i: (0, 0, 0)),
        ),
        compiler_params=params,
        name="span_attention",
    )(received.reshape(owners, slots, CAP, HEADS, HEAD_DIM), prefix_keys, prefix_values)
    part_lse = (
        part_lse.reshape(slots, owners, CAP, HEAD_DIM)
        .transpose(1, 0, 2, 3)
        .reshape(owners, slots * CAP, HEAD_DIM)
    )
    back_lse = lax.all_to_all(part_lse, "owner", split_axis=0, concat_axis=0, tiled=True)
    back_out = lax.all_to_all(
        part_out.reshape(buffer, HEADS, HEAD_DIM), "owner", split_axis=0, concat_axis=0, tiled=True
    )

    tokens = rows * suffix_keys.shape[1]
    head_rows = pl.BlockSpec((rows, heads, HEAD_DIM), lambda i: (0, i, 0))
    suffix_spec = pl.BlockSpec((tokens, cols), lambda i: (0, i))
    out = pl.pallas_call(
        finish_kernel,
        grid=(steps,),
        out_shape=jax.ShapeDtypeStruct((rows, HEADS, HEAD_DIM), jnp.bfloat16),
        in_specs=[
            smem,
            smem,
            smem,
            head_rows,
            suffix_spec,
            suffix_spec,
            pl.BlockSpec((buffer, heads, HEAD_DIM), lambda i: (0, i, 0)),
            pl.BlockSpec((buffer, HEAD_DIM), lambda i: (0, 0)),
        ],
        out_specs=head_rows,
        scratch_shapes=[
            pltpu.SMEM((PREFIXES,), jnp.int32),
            pltpu.VMEM((per_prefix, rows, heads, HEAD_DIM), jnp.bfloat16),
            pltpu.VMEM((per_prefix, rows, HEAD_DIM), jnp.float32),
        ],
        compiler_params=params,
        name="suffix_combine",
    )(
        prefix_ids,
        block_map,
        suffix_len,
        q3,
        suffix_keys.reshape(tokens, width),
        suffix_values.reshape(tokens, width),
        back_out,
        back_lse.reshape(buffer, HEAD_DIM),
    )
    return out.reshape(rows, HEADS * HEAD_DIM)


def solution(mesh):
    placed = (
        P(("groups", "owner"), None),
        P(("groups", "owner"), None),
        P(("groups", "owner")),
        P("groups"),
        P(("groups", "owner"), None, None),
        P(("groups", "owner"), None, None),
        P(("groups", "owner"), None, None),
        P(("groups", "owner"), None, None),
    )
    return jax.shard_map(
        body, mesh=mesh, in_specs=placed, out_specs=P(("groups", "owner"), None), check_vma=False
    )
```

```python
import functools
import math

import jax
import jax.numpy as jnp
from jax import lax
from jax.experimental import pallas as pl
from jax.experimental.pallas import tpu as pltpu
from jax.sharding import PartitionSpec as P

HEADS = 64
KV_HEADS = 8
HEAD_DIM = 128
PREFIXES = 16
CAP = 2
GROUP = HEADS // KV_HEADS
PAIR = 2
FACTOR = 1.0 / math.sqrt(HEAD_DIM)
LOG2E = math.log2(math.e)
NEG_FILL = -1e30
VMEM_LIMIT = 48 * 1024 * 1024


def row_positions(prefix_ref, map_ref, count_ref, rows, per_prefix, visit):
    for p in range(PREFIXES):
        count_ref[p] = 0
    for r in range(rows):
        p = prefix_ref[r]
        rank = count_ref[p]
        count_ref[p] = rank + 1
        for c in range(per_prefix):
            visit(r, c, map_ref[p * per_prefix + c] * CAP + rank)


def dispatch_kernel(prefix_ref, map_ref, q_ref, out_ref, count_ref):
    out_ref[...] = jnp.zeros_like(out_ref)

    def visit(r, c, pos):
        out_ref[pos] = q_ref[r]

    row_positions(
        prefix_ref, map_ref, count_ref, q_ref.shape[0], map_ref.shape[0] // PREFIXES, visit
    )


def span_kernel(q_ref, k_ref, v_ref, out_ref, lse_ref, *, sources, slots, chunk):
    step = pl.program_id(0)

    @pl.when(step == 0)
    def _():
        lse_ref[...] = jnp.zeros_like(lse_ref)

    heads = PAIR * GROUP
    per = chunk * CAP
    for first in range(0, sources, chunk):
        for slot in range(slots):
            q = q_ref[pl.ds(first, chunk), slot].astype(jnp.float32).reshape(per, heads, HEAD_DIM)
            outs = []
            lses = []
            for j in range(PAIR):
                cols = slice(j * HEAD_DIM, (j + 1) * HEAD_DIM)
                qj = q[:, j * GROUP : (j + 1) * GROUP].reshape(per * GROUP, HEAD_DIM)
                raw = lax.dot_general(
                    qj.astype(jnp.bfloat16),
                    k_ref[slot, :, cols],
                    (((1,), (1,)), ((), ())),
                    preferred_element_type=jnp.float32,
                )
                highest = jnp.max(raw, axis=-1, keepdims=True)
                expon = jnp.exp2((raw - highest) * (FACTOR * LOG2E))
                total = jnp.sum(expon, axis=-1, keepdims=True)
                mixed = jnp.dot(
                    expon.astype(jnp.bfloat16),
                    v_ref[slot, :, cols],
                    preferred_element_type=jnp.float32,
                )
                outs.append((mixed / total).reshape(per, GROUP, HEAD_DIM))
                lse = highest * FACTOR + jnp.log(total)
                lses.append(
                    jnp.broadcast_to(lse, (per * GROUP, HEAD_DIM)).reshape(per, GROUP, HEAD_DIM)
                )
            shape = (per, heads, HEAD_DIM)
            out_ref[pl.ds(first, chunk), slot] = (
                jnp.concatenate(outs, axis=1)
                .astype(jnp.bfloat16)
                .reshape(chunk, CAP, heads, HEAD_DIM)
            )
            own = lax.broadcasted_iota(jnp.int32, shape, 2) == (
                lax.broadcasted_iota(jnp.int32, shape, 1) + step * heads
            )
            placed = jnp.sum(jnp.where(own, jnp.concatenate(lses, axis=1), 0.0), axis=1)
            lse_ref[slot, pl.ds(first * CAP, per)] += placed


def finish_kernel(
    prefix_ref,
    map_ref,
    len_ref,
    q_ref,
    sk_ref,
    sv_ref,
    back_ref,
    lse_ref,
    out_ref,
    count_ref,
    sel_ref,
    sel_lse_ref,
):
    step = pl.program_id(0)
    rows = q_ref.shape[0]
    per_prefix = map_ref.shape[0] // PREFIXES
    heads = PAIR * GROUP
    tokens = sk_ref.shape[0]
    room = tokens // rows

    def visit(r, c, pos):
        sel_ref[c, r] = back_ref[pos]
        sel_lse_ref[c, pl.ds(r, 1)] = lse_ref[pl.ds(pos, 1)]

    row_positions(prefix_ref, map_ref, count_ref, rows, per_prefix, visit)

    col = lax.broadcasted_iota(jnp.int32, (1, tokens), 1)
    limit = jnp.zeros((1, tokens), jnp.int32)
    for r in range(rows):
        limit = jnp.where(col // room == r, r * room + len_ref[r], limit)
    owner_row = lax.broadcasted_iota(jnp.int32, (rows * GROUP, tokens), 0) // GROUP
    visible = (owner_row == col // room) & (col < limit)
    q = q_ref[...].astype(jnp.float32)
    results = []
    lane = lax.broadcasted_iota(jnp.int32, (rows, GROUP, HEAD_DIM), 2)
    within = lax.broadcasted_iota(jnp.int32, (rows, GROUP, HEAD_DIM), 1)
    for j in range(PAIR):
        cols = slice(j * HEAD_DIM, (j + 1) * HEAD_DIM)
        part = slice(j * GROUP, (j + 1) * GROUP)
        qj = q[:, part].reshape(rows * GROUP, HEAD_DIM).astype(jnp.bfloat16)
        raw = lax.dot_general(
            qj, sk_ref[:, cols], (((1,), (1,)), ((), ())), preferred_element_type=jnp.float32
        )
        raw = jnp.where(visible, raw, NEG_FILL)
        highest = jnp.max(raw, axis=-1, keepdims=True)
        expon = jnp.where(visible, jnp.exp2((raw - highest) * (FACTOR * LOG2E)), 0.0)
        total = jnp.sum(expon, axis=-1, keepdims=True)
        mixed = jnp.dot(
            expon.astype(jnp.bfloat16), sv_ref[:, cols], preferred_element_type=jnp.float32
        )
        suffix_out = (mixed / total).reshape(rows, GROUP, HEAD_DIM)
        suffix_lse = (highest * FACTOR + jnp.log(total)).reshape(rows, GROUP, 1)
        mine = lane == within + (step * heads + j * GROUP)
        span_lse = []
        top = suffix_lse
        for c in range(per_prefix):
            wide = jnp.broadcast_to(sel_lse_ref[c][:, None, :], (rows, GROUP, HEAD_DIM))
            one = jnp.sum(jnp.where(mine, wide, 0.0), axis=-1, keepdims=True)
            span_lse.append(one)
            top = jnp.maximum(top, one)
        scale = jnp.exp(suffix_lse - top)
        numerator = scale * suffix_out
        denominator = scale
        for c in range(per_prefix):
            scale = jnp.exp(span_lse[c] - top)
            numerator += scale * sel_ref[c].astype(jnp.float32)[:, part]
            denominator += scale
        results.append(numerator / denominator)
    out_ref[...] = jnp.concatenate(results, axis=1).astype(jnp.bfloat16)


def exchange_kernel(*refs, count):
    sources, targets = refs[:count], refs[count : 2 * count]
    send_sem, recv_sem, local_sem = refs[2 * count :]
    me = lax.axis_index("owner")
    n = lax.axis_size("owner")
    barrier = pltpu.get_barrier_semaphore()
    for k in range(1, n):
        pl.semaphore_signal(
            barrier,
            inc=1,
            device_id={"owner": lax.rem(me + k, n)},
            device_id_type=pl.DeviceIdType.MESH,
        )
    own = [
        pltpu.make_async_copy(source.at[me], target.at[me], local_sem.at[a])
        for a, (source, target) in enumerate(zip(sources, targets))
    ]
    for copy in own:
        copy.start()
    pl.semaphore_wait(barrier, n - 1)
    copies = []
    for k in range(1, n):
        peer = lax.rem(me + k, n)
        for a, (source, target) in enumerate(zip(sources, targets)):
            copies.append(
                pltpu.make_async_remote_copy(
                    src_ref=source.at[peer],
                    dst_ref=target.at[me],
                    send_sem=send_sem.at[a, k],
                    recv_sem=recv_sem.at[a, k],
                    device_id={"owner": peer},
                    device_id_type=pl.DeviceIdType.MESH,
                )
            )
            copies[-1].start()
    for copy in own + copies:
        copy.wait()


def exchange(arrays, collective_id, name):
    n = lax.axis_size("owner")
    count = len(arrays)
    anywhere = pl.BlockSpec(memory_space=pl.ANY)
    return pl.pallas_call(
        functools.partial(exchange_kernel, count=count),
        out_shape=tuple(jax.ShapeDtypeStruct(a.shape, a.dtype) for a in arrays),
        in_specs=[anywhere] * count,
        out_specs=(anywhere,) * count,
        scratch_shapes=[
            pltpu.SemaphoreType.DMA((count, n)),
            pltpu.SemaphoreType.DMA((count, n)),
            pltpu.SemaphoreType.DMA((count,)),
        ],
        compiler_params=pltpu.CompilerParams(
            collective_id=collective_id, has_side_effects=True, vmem_limit_bytes=VMEM_LIMIT
        ),
        name=name,
    )(*arrays)


def body(
    queries,
    request_prefix,
    suffix_len,
    block_map,
    prefix_keys,
    prefix_values,
    suffix_keys,
    suffix_values,
):
    owners = lax.axis_size("owner")
    rows = queries.shape[0]
    slot_count = block_map.shape[0]
    slots, span, width = prefix_keys.shape
    per_prefix = slot_count // PREFIXES
    buffer = slot_count * CAP
    heads = PAIR * GROUP
    steps = HEADS // heads
    cols = PAIR * HEAD_DIM
    params = pltpu.CompilerParams(vmem_limit_bytes=VMEM_LIMIT)
    smem = pl.BlockSpec(memory_space=pltpu.SMEM)
    vmem = pl.BlockSpec(memory_space=pltpu.VMEM)
    prefix_ids = request_prefix.reshape(rows)
    q3 = queries.reshape(rows, HEADS, HEAD_DIM)

    outgoing = pl.pallas_call(
        dispatch_kernel,
        out_shape=jax.ShapeDtypeStruct((buffer, HEADS, HEAD_DIM), jnp.bfloat16),
        in_specs=[smem, smem, vmem],
        out_specs=vmem,
        scratch_shapes=[pltpu.SMEM((PREFIXES,), jnp.int32)],
        compiler_params=params,
        name="dispatch",
    )(prefix_ids, block_map, q3)
    (received,) = exchange(
        [outgoing.reshape(owners, slots * CAP, HEADS, HEAD_DIM)], 0, "send_queries"
    )

    chunk = math.gcd(owners, 16)
    block = (owners, slots, CAP, heads, HEAD_DIM)
    row_spec = pl.BlockSpec(block, lambda i: (0, 0, 0, i, 0))
    kv_spec = pl.BlockSpec((slots, span, cols), lambda i: (0, 0, i))
    part_out, part_lse = pl.pallas_call(
        functools.partial(span_kernel, sources=owners, slots=slots, chunk=chunk),
        grid=(steps,),
        out_shape=(
            jax.ShapeDtypeStruct((owners, slots, CAP, HEADS, HEAD_DIM), jnp.bfloat16),
            jax.ShapeDtypeStruct((slots, owners * CAP, HEAD_DIM), jnp.float32),
        ),
        in_specs=[row_spec, kv_spec, kv_spec],
        out_specs=(
            row_spec,
            pl.BlockSpec((slots, owners * CAP, HEAD_DIM), lambda i: (0, 0, 0)),
        ),
        compiler_params=params,
        name="span_attention",
    )(received.reshape(owners, slots, CAP, HEADS, HEAD_DIM), prefix_keys, prefix_values)
    part_lse = (
        part_lse.reshape(slots, owners, CAP, HEAD_DIM)
        .transpose(1, 0, 2, 3)
        .reshape(owners, slots * CAP, HEAD_DIM)
    )
    back_out, back_lse = exchange(
        [part_out.reshape(owners, slots * CAP, HEADS, HEAD_DIM), part_lse], 1, "send_partials"
    )

    tokens = rows * suffix_keys.shape[1]
    head_rows = pl.BlockSpec((rows, heads, HEAD_DIM), lambda i: (0, i, 0))
    suffix_spec = pl.BlockSpec((tokens, cols), lambda i: (0, i))
    out = pl.pallas_call(
        finish_kernel,
        grid=(steps,),
        out_shape=jax.ShapeDtypeStruct((rows, HEADS, HEAD_DIM), jnp.bfloat16),
        in_specs=[
            smem,
            smem,
            smem,
            head_rows,
            suffix_spec,
            suffix_spec,
            pl.BlockSpec((buffer, heads, HEAD_DIM), lambda i: (0, i, 0)),
            pl.BlockSpec((buffer, HEAD_DIM), lambda i: (0, 0)),
        ],
        out_specs=head_rows,
        scratch_shapes=[
            pltpu.SMEM((PREFIXES,), jnp.int32),
            pltpu.VMEM((per_prefix, rows, heads, HEAD_DIM), jnp.bfloat16),
            pltpu.VMEM((per_prefix, rows, HEAD_DIM), jnp.float32),
        ],
        compiler_params=params,
        name="suffix_combine",
    )(
        prefix_ids,
        block_map,
        suffix_len,
        q3,
        suffix_keys.reshape(tokens, width),
        suffix_values.reshape(tokens, width),
        back_out.reshape(buffer, HEADS, HEAD_DIM),
        back_lse.reshape(buffer, HEAD_DIM),
    )
    return out.reshape(rows, HEADS * HEAD_DIM)


def solution(mesh):
    placed = (
        P(("groups", "owner"), None),
        P(("groups", "owner"), None),
        P(("groups", "owner")),
        P("groups"),
        P(("groups", "owner"), None, None),
        P(("groups", "owner"), None, None),
        P(("groups", "owner"), None, None),
        P(("groups", "owner"), None, None),
    )
    return jax.shard_map(
        body, mesh=mesh, in_specs=placed, out_specs=P(("groups", "owner"), None), check_vma=False
    )
```

```python
import functools
import math

import jax
import jax.numpy as jnp
from jax import lax
from jax.experimental import pallas as pl
from jax.experimental.pallas import tpu as pltpu
from jax.sharding import PartitionSpec as P

HEADS = 64
KV_HEADS = 8
HEAD_DIM = 128
PREFIXES = 16
CAP = 2
GROUP = HEADS // KV_HEADS
PAIR = 2
FACTOR = 1.0 / math.sqrt(HEAD_DIM)
LOG2E = math.log2(math.e)
NEG_FILL = -1e30
VMEM_LIMIT = 48 * 1024 * 1024


def row_positions(prefix_ref, map_ref, count_ref, rows, per_prefix, visit):
    for p in range(PREFIXES):
        count_ref[p] = 0
    for r in range(rows):
        p = prefix_ref[r]
        rank = count_ref[p]
        count_ref[p] = rank + 1
        for c in range(per_prefix):
            visit(r, c, map_ref[p * per_prefix + c] * CAP + rank)


def dispatch_kernel(prefix_ref, map_ref, q_ref, out_ref, count_ref):
    out_ref[...] = jnp.zeros_like(out_ref)

    def visit(r, c, pos):
        out_ref[pos] = q_ref[r]

    row_positions(
        prefix_ref, map_ref, count_ref, q_ref.shape[0], map_ref.shape[0] // PREFIXES, visit
    )


def attend_chunk(step, q_ref, k_ref, v_ref, out_ref, lse_ref, chunk):
    sources, slots = q_ref.shape[:2]
    heads = PAIR * GROUP
    per = chunk * CAP
    rows = pl.ds(pl.multiple_of(step * heads, heads), heads)
    for first in range(0, sources, chunk):
        for slot in range(slots):
            q = q_ref[pl.ds(first, chunk), slot, :, rows, :].astype(jnp.float32)
            q = q.reshape(per, heads, HEAD_DIM)
            outs = []
            lses = []
            for j in range(PAIR):
                cols = pl.ds(pl.multiple_of((step * PAIR + j) * HEAD_DIM, HEAD_DIM), HEAD_DIM)
                qj = q[:, j * GROUP : (j + 1) * GROUP].reshape(per * GROUP, HEAD_DIM)
                raw = lax.dot_general(
                    qj.astype(jnp.bfloat16),
                    k_ref[slot, :, cols],
                    (((1,), (1,)), ((), ())),
                    preferred_element_type=jnp.float32,
                )
                highest = jnp.max(raw, axis=-1, keepdims=True)
                expon = jnp.exp2((raw - highest) * (FACTOR * LOG2E))
                total = jnp.sum(expon, axis=-1, keepdims=True)
                mixed = jnp.dot(
                    expon.astype(jnp.bfloat16),
                    v_ref[slot, :, cols],
                    preferred_element_type=jnp.float32,
                )
                outs.append((mixed / total).reshape(per, GROUP, HEAD_DIM))
                lse = highest * FACTOR + jnp.log(total)
                lses.append(
                    jnp.broadcast_to(lse, (per * GROUP, HEAD_DIM)).reshape(per, GROUP, HEAD_DIM)
                )
            shape = (chunk, CAP, heads, HEAD_DIM)
            out_ref[pl.ds(first, chunk), slot, :, rows, :] = (
                jnp.concatenate(outs, axis=1).astype(jnp.bfloat16).reshape(shape)
            )
            own = lax.broadcasted_iota(jnp.int32, shape, 3) == (
                lax.broadcasted_iota(jnp.int32, shape, 2) + step * heads
            )
            lses = jnp.concatenate(lses, axis=1).reshape(shape)
            lse_ref[pl.ds(first, chunk), slot] += jnp.sum(
                jnp.where(own, lses, 0.0), axis=2, keepdims=True
            )


def span_kernel(
    ask_ref,
    k_hbm,
    v_hbm,
    back_ref,
    back_lse_ref,
    q_ref,
    k_ref,
    v_ref,
    out_ref,
    lse_ref,
    kv_sem,
    own_sem,
    ask_send,
    ask_recv,
    back_send,
    back_recv,
    lse_send,
    lse_recv,
    *,
    chunk,
):
    me = lax.axis_index("owner")
    n = lax.axis_size("owner")
    heads = PAIR * GROUP
    steps = HEADS // heads

    def remote(source, target, send_sem, recv_sem, peer):
        return pltpu.make_async_remote_copy(
            src_ref=source,
            dst_ref=target,
            send_sem=send_sem,
            recv_sem=recv_sem,
            device_id={"owner": peer},
            device_id_type=pl.DeviceIdType.MESH,
        )

    def peer_of(k):
        return lax.rem(me + k, n)

    def part(ref, who, step):
        return ref.at[who, :, :, pl.ds(pl.multiple_of(step * heads, heads), heads), :]

    def ask(step, k):
        peer = peer_of(k)
        return remote(
            part(ask_ref, peer, step),
            part(q_ref, me, step),
            ask_send.at[step, k],
            ask_recv.at[step, k],
            peer,
        )

    def answer(step, k):
        peer = peer_of(k)
        return remote(
            part(out_ref, peer, step),
            part(back_ref, me, step),
            back_send.at[step, k],
            back_recv.at[step, k],
            peer,
        )

    def answer_lse(k):
        peer = peer_of(k)
        return remote(lse_ref.at[peer], back_lse_ref.at[me], lse_send.at[k], lse_recv.at[k], peer)

    def load(step):
        cols = pl.ds(pl.multiple_of(step * PAIR * HEAD_DIM, HEAD_DIM), PAIR * HEAD_DIM)
        return [
            pltpu.make_async_copy(k_hbm.at[:, :, cols], k_ref.at[:, :, cols], kv_sem.at[0, step]),
            pltpu.make_async_copy(v_hbm.at[:, :, cols], v_ref.at[:, :, cols], kv_sem.at[1, step]),
        ]

    own_ask = pltpu.make_async_copy(ask_ref.at[me], q_ref.at[me], own_sem.at[0])
    own_out = pltpu.make_async_copy(out_ref.at[me], back_ref.at[me], own_sem.at[1])
    own_lse = pltpu.make_async_copy(lse_ref.at[me], back_lse_ref.at[me], own_sem.at[2])

    barrier = pltpu.get_barrier_semaphore()
    for k in range(1, n):
        pl.semaphore_signal(
            barrier,
            inc=1,
            device_id={"owner": peer_of(k)},
            device_id_type=pl.DeviceIdType.MESH,
        )
    own_ask.start()
    lse_ref[...] = jnp.zeros_like(lse_ref)
    pl.semaphore_wait(barrier, n - 1)

    @pl.loop(0, steps)
    def _(step):
        for k in range(1, n):
            ask(step, k).start()
        for copy in load(step):
            copy.start()

    own_ask.wait()

    @pl.loop(0, steps)
    def _(step):
        for copy in load(step):
            copy.wait()
        for k in range(1, n):
            ask(step, k).wait_recv()
        attend_chunk(step, q_ref, k_ref, v_ref, out_ref, lse_ref, chunk)
        for k in range(1, n):
            answer(step, k).start()

    own_out.start()
    own_lse.start()
    for k in range(1, n):
        answer_lse(k).start()

    @pl.loop(0, steps)
    def _(step):
        for k in range(1, n):
            ask(step, k).wait_send()
            answer(step, k).wait()

    for k in range(1, n):
        answer_lse(k).wait()
    own_out.wait()
    own_lse.wait()


def finish_kernel(
    prefix_ref,
    map_ref,
    len_ref,
    q_ref,
    sk_ref,
    sv_ref,
    back_ref,
    lse_ref,
    out_ref,
    count_ref,
    sel_ref,
    sel_lse_ref,
):
    step = pl.program_id(0)
    rows = q_ref.shape[0]
    per_prefix = map_ref.shape[0] // PREFIXES
    heads = PAIR * GROUP
    tokens = sk_ref.shape[0]
    room = tokens // rows

    def visit(r, c, pos):
        sel_ref[c, r] = back_ref[pos]
        sel_lse_ref[c, pl.ds(r, 1)] = lse_ref[pos]

    row_positions(prefix_ref, map_ref, count_ref, rows, per_prefix, visit)

    col = lax.broadcasted_iota(jnp.int32, (1, tokens), 1)
    limit = jnp.zeros((1, tokens), jnp.int32)
    for r in range(rows):
        limit = jnp.where(col // room == r, r * room + len_ref[r], limit)
    owner_row = lax.broadcasted_iota(jnp.int32, (rows * GROUP, tokens), 0) // GROUP
    visible = (owner_row == col // room) & (col < limit)
    q = q_ref[...].astype(jnp.float32)
    results = []
    lane = lax.broadcasted_iota(jnp.int32, (rows, GROUP, HEAD_DIM), 2)
    within = lax.broadcasted_iota(jnp.int32, (rows, GROUP, HEAD_DIM), 1)
    for j in range(PAIR):
        cols = slice(j * HEAD_DIM, (j + 1) * HEAD_DIM)
        part = slice(j * GROUP, (j + 1) * GROUP)
        qj = q[:, part].reshape(rows * GROUP, HEAD_DIM).astype(jnp.bfloat16)
        raw = lax.dot_general(
            qj, sk_ref[:, cols], (((1,), (1,)), ((), ())), preferred_element_type=jnp.float32
        )
        raw = jnp.where(visible, raw, NEG_FILL)
        highest = jnp.max(raw, axis=-1, keepdims=True)
        expon = jnp.where(visible, jnp.exp2((raw - highest) * (FACTOR * LOG2E)), 0.0)
        total = jnp.sum(expon, axis=-1, keepdims=True)
        mixed = jnp.dot(
            expon.astype(jnp.bfloat16), sv_ref[:, cols], preferred_element_type=jnp.float32
        )
        suffix_out = (mixed / total).reshape(rows, GROUP, HEAD_DIM)
        suffix_lse = (highest * FACTOR + jnp.log(total)).reshape(rows, GROUP, 1)
        mine = lane == within + (step * heads + j * GROUP)
        span_lse = []
        top = suffix_lse
        for c in range(per_prefix):
            wide = jnp.broadcast_to(sel_lse_ref[c][:, None, :], (rows, GROUP, HEAD_DIM))
            one = jnp.sum(jnp.where(mine, wide, 0.0), axis=-1, keepdims=True)
            span_lse.append(one)
            top = jnp.maximum(top, one)
        scale = jnp.exp(suffix_lse - top)
        numerator = scale * suffix_out
        denominator = scale
        for c in range(per_prefix):
            scale = jnp.exp(span_lse[c] - top)
            numerator += scale * sel_ref[c].astype(jnp.float32)[:, part]
            denominator += scale
        results.append(numerator / denominator)
    out_ref[...] = jnp.concatenate(results, axis=1).astype(jnp.bfloat16)


def body(
    queries,
    request_prefix,
    suffix_len,
    block_map,
    prefix_keys,
    prefix_values,
    suffix_keys,
    suffix_values,
):
    owners = lax.axis_size("owner")
    rows = queries.shape[0]
    slot_count = block_map.shape[0]
    slots, _, width = prefix_keys.shape
    per_prefix = slot_count // PREFIXES
    buffer = slot_count * CAP
    heads = PAIR * GROUP
    steps = HEADS // heads
    cols = PAIR * HEAD_DIM
    params = pltpu.CompilerParams(vmem_limit_bytes=VMEM_LIMIT)
    smem = pl.BlockSpec(memory_space=pltpu.SMEM)
    vmem = pl.BlockSpec(memory_space=pltpu.VMEM)
    prefix_ids = request_prefix.reshape(rows)
    q3 = queries.reshape(rows, HEADS, HEAD_DIM)

    outgoing = pl.pallas_call(
        dispatch_kernel,
        out_shape=jax.ShapeDtypeStruct((buffer, HEADS, HEAD_DIM), jnp.bfloat16),
        in_specs=[smem, smem, vmem],
        out_specs=vmem,
        scratch_shapes=[pltpu.SMEM((PREFIXES,), jnp.int32)],
        compiler_params=params,
        name="dispatch",
    )(prefix_ids, block_map, q3)
    chunk = math.gcd(owners, 16)
    items = (owners, slots, CAP, HEADS, HEAD_DIM)
    lses = (owners, slots, CAP, 1, HEAD_DIM)
    anywhere = pl.BlockSpec(memory_space=pl.ANY)
    back_out, back_lse = pl.pallas_call(
        functools.partial(span_kernel, chunk=chunk),
        out_shape=(
            jax.ShapeDtypeStruct(items, jnp.bfloat16),
            jax.ShapeDtypeStruct(lses, jnp.float32),
        ),
        in_specs=[anywhere] * 3,
        out_specs=(anywhere, anywhere),
        scratch_shapes=[
            pltpu.VMEM(items, jnp.bfloat16),
            pltpu.VMEM(prefix_keys.shape, jnp.bfloat16),
            pltpu.VMEM(prefix_values.shape, jnp.bfloat16),
            pltpu.VMEM(items, jnp.bfloat16),
            pltpu.VMEM(lses, jnp.float32),
            pltpu.SemaphoreType.DMA((2, steps)),
            pltpu.SemaphoreType.DMA((3,)),
            pltpu.SemaphoreType.DMA((steps, owners)),
            pltpu.SemaphoreType.DMA((steps, owners)),
            pltpu.SemaphoreType.DMA((steps, owners)),
            pltpu.SemaphoreType.DMA((steps, owners)),
            pltpu.SemaphoreType.DMA((owners,)),
            pltpu.SemaphoreType.DMA((owners,)),
        ],
        compiler_params=pltpu.CompilerParams(
            collective_id=0, has_side_effects=True, vmem_limit_bytes=VMEM_LIMIT
        ),
        name="span_attention",
    )(outgoing.reshape(items), prefix_keys, prefix_values)

    tokens = rows * suffix_keys.shape[1]
    head_rows = pl.BlockSpec((rows, heads, HEAD_DIM), lambda i: (0, i, 0))
    suffix_spec = pl.BlockSpec((tokens, cols), lambda i: (0, i))
    out = pl.pallas_call(
        finish_kernel,
        grid=(steps,),
        out_shape=jax.ShapeDtypeStruct((rows, HEADS, HEAD_DIM), jnp.bfloat16),
        in_specs=[
            smem,
            smem,
            smem,
            head_rows,
            suffix_spec,
            suffix_spec,
            pl.BlockSpec((buffer, heads, HEAD_DIM), lambda i: (0, i, 0)),
            pl.BlockSpec((buffer, 1, HEAD_DIM), lambda i: (0, 0, 0)),
        ],
        out_specs=head_rows,
        scratch_shapes=[
            pltpu.SMEM((PREFIXES,), jnp.int32),
            pltpu.VMEM((per_prefix, rows, heads, HEAD_DIM), jnp.bfloat16),
            pltpu.VMEM((per_prefix, rows, HEAD_DIM), jnp.float32),
        ],
        compiler_params=params,
        name="suffix_combine",
    )(
        prefix_ids,
        block_map,
        suffix_len,
        q3,
        suffix_keys.reshape(tokens, width),
        suffix_values.reshape(tokens, width),
        back_out.reshape(buffer, HEADS, HEAD_DIM),
        back_lse.reshape(buffer, 1, HEAD_DIM),
    )
    return out.reshape(rows, HEADS * HEAD_DIM)


def solution(mesh):
    placed = (
        P(("groups", "owner"), None),
        P(("groups", "owner"), None),
        P(("groups", "owner")),
        P("groups"),
        P(("groups", "owner"), None, None),
        P(("groups", "owner"), None, None),
        P(("groups", "owner"), None, None),
        P(("groups", "owner"), None, None),
    )
    return jax.shard_map(
        body, mesh=mesh, in_specs=placed, out_specs=P(("groups", "owner"), None), check_vma=False
    )
```

```python
import functools
import math

import jax
import jax.numpy as jnp
from jax import lax
from jax.experimental import pallas as pl
from jax.experimental.pallas import tpu as pltpu
from jax.sharding import PartitionSpec as P

HEADS = 64
KV_HEADS = 8
HEAD_DIM = 128
PREFIXES = 16
CAP = 2
GROUP = HEADS // KV_HEADS
PAIR = 2
FACTOR = 1.0 / math.sqrt(HEAD_DIM)
LOG2E = math.log2(math.e)
NEG_FILL = -1e30
VMEM_LIMIT = 48 * 1024 * 1024


def row_positions(prefix_ref, map_ref, count_ref, rows, per_prefix, visit):
    for p in range(PREFIXES):
        count_ref[p] = 0
    for r in range(rows):
        p = prefix_ref[r]
        rank = count_ref[p]
        count_ref[p] = rank + 1
        for c in range(per_prefix):
            visit(r, c, map_ref[p * per_prefix + c] * CAP + rank)


def dispatch_kernel(prefix_ref, map_ref, q_ref, out_ref, count_ref):
    out_ref[...] = jnp.zeros_like(out_ref)

    def visit(r, c, pos):
        out_ref[pos] = q_ref[r]

    row_positions(
        prefix_ref, map_ref, count_ref, q_ref.shape[0], map_ref.shape[0] // PREFIXES, visit
    )


def attend_chunk(step, q_ref, k_ref, v_ref, out_ref, lse_ref, chunk):
    sources, slots = q_ref.shape[:2]
    heads = PAIR * GROUP
    per = chunk * CAP
    rows = pl.ds(pl.multiple_of(step * heads, heads), heads)
    for first in range(0, sources, chunk):
        for slot in range(slots):
            q = q_ref[pl.ds(first, chunk), slot, :, rows, :].astype(jnp.float32)
            q = q.reshape(per, heads, HEAD_DIM)
            outs = []
            lses = []
            for j in range(PAIR):
                cols = pl.ds(pl.multiple_of((step * PAIR + j) * HEAD_DIM, HEAD_DIM), HEAD_DIM)
                qj = q[:, j * GROUP : (j + 1) * GROUP].reshape(per * GROUP, HEAD_DIM)
                raw = lax.dot_general(
                    qj.astype(jnp.bfloat16),
                    k_ref[slot, :, cols],
                    (((1,), (1,)), ((), ())),
                    preferred_element_type=jnp.float32,
                )
                highest = jnp.max(raw, axis=-1, keepdims=True)
                expon = jnp.exp2((raw - highest) * (FACTOR * LOG2E))
                total = jnp.sum(expon, axis=-1, keepdims=True)
                mixed = jnp.dot(
                    expon.astype(jnp.bfloat16),
                    v_ref[slot, :, cols],
                    preferred_element_type=jnp.float32,
                )
                outs.append((mixed / total).reshape(per, GROUP, HEAD_DIM))
                lse = highest * FACTOR + jnp.log(total)
                lses.append(
                    jnp.broadcast_to(lse, (per * GROUP, HEAD_DIM)).reshape(per, GROUP, HEAD_DIM)
                )
            shape = (chunk, CAP, heads, HEAD_DIM)
            out_ref[pl.ds(first, chunk), slot, :, rows, :] = (
                jnp.concatenate(outs, axis=1).astype(jnp.bfloat16).reshape(shape)
            )
            own = lax.broadcasted_iota(jnp.int32, shape, 3) == (
                lax.broadcasted_iota(jnp.int32, shape, 2) + step * heads
            )
            lses = jnp.concatenate(lses, axis=1).reshape(shape)
            lse_ref[pl.ds(first, chunk), slot] += jnp.sum(
                jnp.where(own, lses, 0.0), axis=2, keepdims=True
            )


def attend_suffix(len_ref, q_ref, sk_ref, sv_ref, out_ref, lse_ref):
    rows = q_ref.shape[0]
    tokens = sk_ref.shape[0]
    room = tokens // rows
    col = lax.broadcasted_iota(jnp.int32, (1, tokens), 1)
    limit = jnp.zeros((1, tokens), jnp.int32)
    for r in range(rows):
        limit = jnp.where(col // room == r, r * room + len_ref[r], limit)
    owner_row = lax.broadcasted_iota(jnp.int32, (rows * GROUP, tokens), 0) // GROUP
    visible = (owner_row == col // room) & (col < limit)
    q = q_ref[...].astype(jnp.float32)
    for j in range(KV_HEADS):
        cols = slice(j * HEAD_DIM, (j + 1) * HEAD_DIM)
        part = slice(j * GROUP, (j + 1) * GROUP)
        qj = q[:, part].reshape(rows * GROUP, HEAD_DIM).astype(jnp.bfloat16)
        raw = lax.dot_general(
            qj, sk_ref[:, cols], (((1,), (1,)), ((), ())), preferred_element_type=jnp.float32
        )
        raw = jnp.where(visible, raw, NEG_FILL)
        highest = jnp.max(raw, axis=-1, keepdims=True)
        expon = jnp.where(visible, jnp.exp2((raw - highest) * (FACTOR * LOG2E)), 0.0)
        total = jnp.sum(expon, axis=-1, keepdims=True)
        mixed = jnp.dot(
            expon.astype(jnp.bfloat16), sv_ref[:, cols], preferred_element_type=jnp.float32
        )
        out_ref[:, part] = (mixed / total).reshape(rows, GROUP, HEAD_DIM)
        lse = jnp.broadcast_to(highest * FACTOR + jnp.log(total), (rows * GROUP, HEAD_DIM))
        lse_ref[:, part] = lse.reshape(rows, GROUP, HEAD_DIM)


def span_kernel(
    ask_ref,
    k_hbm,
    v_hbm,
    len_ref,
    own_q_ref,
    sk_ref,
    sv_ref,
    back_ref,
    back_lse_ref,
    suf_ref,
    suf_lse_ref,
    q_ref,
    k_ref,
    v_ref,
    out_ref,
    lse_ref,
    kv_sem,
    own_sem,
    ask_send,
    ask_recv,
    back_send,
    back_recv,
    lse_send,
    lse_recv,
    *,
    chunk,
):
    me = lax.axis_index("owner")
    n = lax.axis_size("owner")
    heads = PAIR * GROUP
    steps = HEADS // heads

    def remote(source, target, send_sem, recv_sem, peer):
        return pltpu.make_async_remote_copy(
            src_ref=source,
            dst_ref=target,
            send_sem=send_sem,
            recv_sem=recv_sem,
            device_id={"owner": peer},
            device_id_type=pl.DeviceIdType.MESH,
        )

    def peer_of(k):
        return lax.rem(me + k, n)

    def part(ref, who, step):
        return ref.at[who, :, :, pl.ds(pl.multiple_of(step * heads, heads), heads), :]

    def ask(step, k):
        peer = peer_of(k)
        return remote(
            part(ask_ref, peer, step),
            part(q_ref, me, step),
            ask_send.at[step, k],
            ask_recv.at[step, k],
            peer,
        )

    def answer(step, k):
        peer = peer_of(k)
        return remote(
            part(out_ref, peer, step),
            part(back_ref, me, step),
            back_send.at[step, k],
            back_recv.at[step, k],
            peer,
        )

    def answer_lse(k):
        peer = peer_of(k)
        return remote(lse_ref.at[peer], back_lse_ref.at[me], lse_send.at[k], lse_recv.at[k], peer)

    def load(step):
        cols = pl.ds(pl.multiple_of(step * PAIR * HEAD_DIM, HEAD_DIM), PAIR * HEAD_DIM)
        return [
            pltpu.make_async_copy(k_hbm.at[:, :, cols], k_ref.at[:, :, cols], kv_sem.at[0, step]),
            pltpu.make_async_copy(v_hbm.at[:, :, cols], v_ref.at[:, :, cols], kv_sem.at[1, step]),
        ]

    own_ask = pltpu.make_async_copy(ask_ref.at[me], q_ref.at[me], own_sem.at[0])
    own_out = pltpu.make_async_copy(out_ref.at[me], back_ref.at[me], own_sem.at[1])
    own_lse = pltpu.make_async_copy(lse_ref.at[me], back_lse_ref.at[me], own_sem.at[2])

    barrier = pltpu.get_barrier_semaphore()
    for k in range(1, n):
        pl.semaphore_signal(
            barrier,
            inc=1,
            device_id={"owner": peer_of(k)},
            device_id_type=pl.DeviceIdType.MESH,
        )
    own_ask.start()
    lse_ref[...] = jnp.zeros_like(lse_ref)
    pl.semaphore_wait(barrier, n - 1)

    @pl.loop(0, steps)
    def _(step):
        for k in range(1, n):
            ask(step, k).start()
        for copy in load(step):
            copy.start()

    attend_suffix(len_ref, own_q_ref, sk_ref, sv_ref, suf_ref, suf_lse_ref)
    own_ask.wait()

    @pl.loop(0, steps)
    def _(step):
        for copy in load(step):
            copy.wait()
        for k in range(1, n):
            ask(step, k).wait_recv()
        attend_chunk(step, q_ref, k_ref, v_ref, out_ref, lse_ref, chunk)
        for k in range(1, n):
            answer(step, k).start()

    own_out.start()
    own_lse.start()
    for k in range(1, n):
        answer_lse(k).start()

    @pl.loop(0, steps)
    def _(step):
        for k in range(1, n):
            ask(step, k).wait_send()
            answer(step, k).wait()

    for k in range(1, n):
        answer_lse(k).wait()
    own_out.wait()
    own_lse.wait()


def finish_kernel(
    prefix_ref,
    map_ref,
    suf_ref,
    suf_lse_ref,
    back_ref,
    lse_ref,
    out_ref,
    count_ref,
    sel_ref,
    sel_lse_ref,
):
    step = pl.program_id(0)
    rows = suf_ref.shape[0]
    per_prefix = map_ref.shape[0] // PREFIXES
    heads = PAIR * GROUP

    def visit(r, c, pos):
        sel_ref[c, r] = back_ref[pos]
        sel_lse_ref[c, pl.ds(r, 1)] = lse_ref[pos]

    row_positions(prefix_ref, map_ref, count_ref, rows, per_prefix, visit)

    results = []
    lane = lax.broadcasted_iota(jnp.int32, (rows, GROUP, HEAD_DIM), 2)
    within = lax.broadcasted_iota(jnp.int32, (rows, GROUP, HEAD_DIM), 1)
    for j in range(PAIR):
        part = slice(j * GROUP, (j + 1) * GROUP)
        suffix_out, suffix_lse = suf_ref[:, part], suf_lse_ref[:, part]
        mine = lane == within + (step * heads + j * GROUP)
        span_lse = []
        top = suffix_lse
        for c in range(per_prefix):
            wide = jnp.broadcast_to(sel_lse_ref[c][:, None, :], (rows, GROUP, HEAD_DIM))
            one = jnp.sum(jnp.where(mine, wide, 0.0), axis=-1, keepdims=True)
            span_lse.append(one)
            top = jnp.maximum(top, one)
        scale = jnp.exp(suffix_lse - top)
        numerator = scale * suffix_out
        denominator = scale
        for c in range(per_prefix):
            scale = jnp.exp(span_lse[c] - top)
            numerator += scale * sel_ref[c].astype(jnp.float32)[:, part]
            denominator += scale
        results.append(numerator / denominator)
    out_ref[...] = jnp.concatenate(results, axis=1).astype(jnp.bfloat16)


def body(
    queries,
    request_prefix,
    suffix_len,
    block_map,
    prefix_keys,
    prefix_values,
    suffix_keys,
    suffix_values,
):
    owners = lax.axis_size("owner")
    rows = queries.shape[0]
    slot_count = block_map.shape[0]
    slots, _, width = prefix_keys.shape
    per_prefix = slot_count // PREFIXES
    buffer = slot_count * CAP
    heads = PAIR * GROUP
    steps = HEADS // heads
    params = pltpu.CompilerParams(vmem_limit_bytes=VMEM_LIMIT)
    smem = pl.BlockSpec(memory_space=pltpu.SMEM)
    vmem = pl.BlockSpec(memory_space=pltpu.VMEM)
    prefix_ids = request_prefix.reshape(rows)
    q3 = queries.reshape(rows, HEADS, HEAD_DIM)

    outgoing = pl.pallas_call(
        dispatch_kernel,
        out_shape=jax.ShapeDtypeStruct((buffer, HEADS, HEAD_DIM), jnp.bfloat16),
        in_specs=[smem, smem, vmem],
        out_specs=vmem,
        scratch_shapes=[pltpu.SMEM((PREFIXES,), jnp.int32)],
        compiler_params=params,
        name="dispatch",
    )(prefix_ids, block_map, q3)
    chunk = math.gcd(owners, 16)
    items = (owners, slots, CAP, HEADS, HEAD_DIM)
    lses = (owners, slots, CAP, 1, HEAD_DIM)
    anywhere = pl.BlockSpec(memory_space=pl.ANY)
    tokens = rows * suffix_keys.shape[1]
    suffix = jax.ShapeDtypeStruct((rows, HEADS, HEAD_DIM), jnp.float32)
    back_out, back_lse, suf_out, suf_lse = pl.pallas_call(
        functools.partial(span_kernel, chunk=chunk),
        out_shape=(
            jax.ShapeDtypeStruct(items, jnp.bfloat16),
            jax.ShapeDtypeStruct(lses, jnp.float32),
            suffix,
            suffix,
        ),
        in_specs=[anywhere] * 3 + [smem, vmem, vmem, vmem],
        out_specs=(anywhere, anywhere, vmem, vmem),
        scratch_shapes=[
            pltpu.VMEM(items, jnp.bfloat16),
            pltpu.VMEM(prefix_keys.shape, jnp.bfloat16),
            pltpu.VMEM(prefix_values.shape, jnp.bfloat16),
            pltpu.VMEM(items, jnp.bfloat16),
            pltpu.VMEM(lses, jnp.float32),
            pltpu.SemaphoreType.DMA((2, steps)),
            pltpu.SemaphoreType.DMA((3,)),
            pltpu.SemaphoreType.DMA((steps, owners)),
            pltpu.SemaphoreType.DMA((steps, owners)),
            pltpu.SemaphoreType.DMA((steps, owners)),
            pltpu.SemaphoreType.DMA((steps, owners)),
            pltpu.SemaphoreType.DMA((owners,)),
            pltpu.SemaphoreType.DMA((owners,)),
        ],
        compiler_params=pltpu.CompilerParams(
            collective_id=0, has_side_effects=True, vmem_limit_bytes=VMEM_LIMIT
        ),
        name="span_attention",
    )(
        outgoing.reshape(items),
        prefix_keys,
        prefix_values,
        suffix_len,
        q3,
        suffix_keys.reshape(tokens, width),
        suffix_values.reshape(tokens, width),
    )

    head_rows = pl.BlockSpec((rows, heads, HEAD_DIM), lambda i: (0, i, 0))
    out = pl.pallas_call(
        finish_kernel,
        grid=(steps,),
        out_shape=jax.ShapeDtypeStruct((rows, HEADS, HEAD_DIM), jnp.bfloat16),
        in_specs=[
            smem,
            smem,
            head_rows,
            head_rows,
            pl.BlockSpec((buffer, heads, HEAD_DIM), lambda i: (0, i, 0)),
            pl.BlockSpec((buffer, 1, HEAD_DIM), lambda i: (0, 0, 0)),
        ],
        out_specs=head_rows,
        scratch_shapes=[
            pltpu.SMEM((PREFIXES,), jnp.int32),
            pltpu.VMEM((per_prefix, rows, heads, HEAD_DIM), jnp.bfloat16),
            pltpu.VMEM((per_prefix, rows, HEAD_DIM), jnp.float32),
        ],
        compiler_params=params,
        name="suffix_combine",
    )(
        prefix_ids,
        block_map,
        suf_out,
        suf_lse,
        back_out.reshape(buffer, HEADS, HEAD_DIM),
        back_lse.reshape(buffer, 1, HEAD_DIM),
    )
    return out.reshape(rows, HEADS * HEAD_DIM)


def solution(mesh):
    placed = (
        P(("groups", "owner"), None),
        P(("groups", "owner"), None),
        P(("groups", "owner")),
        P("groups"),
        P(("groups", "owner"), None, None),
        P(("groups", "owner"), None, None),
        P(("groups", "owner"), None, None),
        P(("groups", "owner"), None, None),
    )
    return jax.shard_map(
        body, mesh=mesh, in_specs=placed, out_specs=P(("groups", "owner"), None), check_vma=False
    )
```
